32 devices in a mesh: seq: 4 (over x, core), batch: 8 (over z, y).
Axes of the slice: x: 2, y: 2, z: 4, core: 2. Of those that a mesh axis runs over, the one named last changes fastest.
Arguments:
- tokens: bfloat16 [8, 512, 2048], P('batch', 'seq'), may hold values from -6 to 6
- lengths: int32 [8], P('batch'), may hold values from 1 to 512, 2560 in all
- cotangent: bfloat16 [8, 512, 2048], P('batch', 'seq'), may hold values from -6 to 6
- input_proj: bfloat16 [2048, 2560], P(('seq', 'batch')), may hold values from -0.125 to 0.125
- branch_proj: bfloat16 [2048, 2560], P(('seq', 'batch')), may hold values from -0.125 to 0.125
- output_proj: bfloat16 [2560, 2048], P(('seq', 'batch')), may hold values from -0.3125 to 0.3125
- recur_gate: bfloat16 [2560, 256], P(('seq', 'batch')), may hold values from -0.375 to 0.375
- inlet_gate: bfloat16 [2560, 256], P(('seq', 'batch')), may hold values from -0.375 to 0.375
- conv_kernel: bfloat16 [4, 2560], P(None, ('seq', 'batch')), may hold values from -3 to 3
- conv_bias: bfloat16 [2560], P(('seq', 'batch')), may hold values from -3 to 3
- recur_bias: bfloat16 [2560], P(('seq', 'batch')), may hold values from -4 to 4
- inlet_bias: bfloat16 [2560], P(('seq', 'batch')), may hold values from -4 to 4
- decay_param: bfloat16 [2560], P(('seq', 'batch')), may hold values from -12 to -4
- mixer_gain: bfloat16 [2048], P(('seq', 'batch')), may hold values from 0.5 to 1.5
- feed_gain: bfloat16 [2048], P(('seq', 'batch')), may hold values from 0.5 to 1.5
- feed_gate: bfloat16 [2048, 6144], P('batch', 'seq'), may hold values from -0.125 to 0.125
- feed_up: bfloat16 [2048, 6144], P('batch', 'seq'), may hold values from -0.125 to 0.125
- feed_down: bfloat16 [6144, 2048], P('seq', 'batch'), may hold values from -0.078125 to 0.078125
Outputs:
- output: bfloat16 [8, 512, 2048], P('batch', 'seq')
- grad_tokens: float32 [8, 512, 2048], P('batch', 'seq')
- grad_input_proj: float32 [2048, 2560], P(('seq', 'batch'))
- grad_branch_proj: float32 [2048, 2560], P(('seq', 'batch'))
- grad_output_proj: float32 [2560, 2048], P(('seq', 'batch'))
- grad_recur_gate: float32 [2560, 256], P(('seq', 'batch'))
- grad_inlet_gate: float32 [2560, 256], P(('seq', 'batch'))
- grad_conv_kernel: float32 [4, 2560], P(None, ('seq', 'batch'))
- grad_conv_bias: float32 [2560], P(('seq', 'batch'))
- grad_recur_bias: float32 [2560], P(('seq', 'batch'))
- grad_inlet_bias: float32 [2560], P(('seq', 'batch'))
- grad_decay_param: float32 [2560], P(('seq', 'batch'))
- grad_mixer_gain: float32 [2048], P(('seq', 'batch'))
- grad_feed_gain: float32 [2048], P(('seq', 'batch'))
- grad_feed_gate: float32 [2048, 6144], P('batch', 'seq')
- grad_feed_up: float32 [2048, 6144], P('batch', 'seq')
- grad_feed_down: float32 [6144, 2048], P('seq', 'batch')
The draws below stay inside these ranges and needn't reach their ends.
All inputs are finite; a program needn't handle non-finite values. No bound on the sum of `lengths` on one device may be relied on, other than what follows from the above.
Results may differ from the reference program's by a relative error of at most 0.014.
Values may be sent and summed in bfloat16 or wider, within the bound.
No kernel may reach another device: no remote copies, remote signals or barrier semaphores. Data moves between devices by JAX's collectives and lax.ppermute only.
A program may use at most 320 MiB of HBM per device.

```python
import math
from functools import partial
import jax
import jax.numpy as jnp
import numpy as np
from jax import lax

D = 2048
NH = 10
HB = 256
FF = 6144
RNN_WIDTH = 2560
LENGTH = 512
SEQS = 8


def draw_decay_param(key, part):
    channels = NH * HB
    rates = jnp.exp(jax.random.uniform(jax.random.fold_in(key, 4), (channels,), jnp.float32, jnp.log(0.05 / LENGTH), jnp.log(0.015)))
    return jnp.log(jnp.expm1(rates)).astype(jnp.bfloat16)


def levels(stream_key, extent, split, low, high):
    def one(position, blocks):
        draws = jax.random.uniform(jax.random.fold_in(jax.random.fold_in(stream_key, 6), position), (blocks,), jnp.float32, low / len(split), high / len(split))
        return jnp.repeat(jnp.exp(draws), extent[position] // blocks).reshape((-1,) + (1,) * (len(extent) - position - 1))

    level = one(*split[0])
    for cut in split[1:]:
        level = level * one(*cut)
    return level


def split_up(amount, total, reach, skew):
    portions = [(1 << 20) // math.isqrt(grade ** skew) + 1 for grade in range(2, amount + 1)]
    surplus, given = total - reach - (amount - 1), [1] * (amount - 1)
    while surplus > 0:
        movable = [i for i in range(amount - 1) if given[i] < reach]
        mass, left = sum([portions[i] for i in movable]), surplus
        for i in movable:
            addition = min(reach - given[i], max(1, left * portions[i] // mass), surplus)
            given[i] = given[i] + addition
            surplus = surplus - addition
    return np.array([reach] + given)


def ragged_sizes(rng, number_of, total, most, slope):
    if number_of == 2:
        one = jax.random.randint(rng, (), max(1, total - most), min(most, total - 1) + 1)
        return jnp.stack([one, total - one])
    tallies = jnp.asarray(split_up(number_of, total, most, slope), jnp.int32)
    twos = (number_of - 1) // 2
    donor, sink = tallies[1:1 + 2 * twos:2], tallies[2:2 + 2 * twos:2]
    room = jnp.minimum(donor - 1, most - sink)
    shifted = jax.random.randint(jax.random.fold_in(rng, 1), (twos,), 0, 1 << 20) % (room + 1)
    tallies = tallies.at[1:1 + 2 * twos:2].set(donor - shifted).at[2:2 + 2 * twos:2].set(sink + shifted)
    return tallies[jax.random.permutation(jax.random.fold_in(rng, 2), number_of)]


def noise(key, extent, scale, bound, pieces=(), kind=jnp.bfloat16):
    values = jax.random.normal(key, extent, jnp.float32) * scale
    if len(pieces) > 0:
        values = levels(key, extent, pieces, -0.22, 0.18) * values
    return jnp.clip(values, min=-bound, max=bound).astype(kind)


def setup_inputs(seed: int = 0) -> dict:
    seeds = jax.random.split(jax.random.key(seed), 19)
    tokens = noise(seeds[0], (SEQS, LENGTH, D), 1.0, 6.0, ((0, 8), (1, 4)))
    lengths = ragged_sizes(seeds[1], SEQS, SEQS * LENGTH * 5 // 8, LENGTH, 2).astype(jnp.int32)
    cotangent = noise(seeds[2], (SEQS, LENGTH, D), 1.0, 6.0, ((0, 8), (1, 4)))
    input_proj = noise(seeds[3], (D, RNN_WIDTH), D ** -0.5, 0.125, ((0, 32),))
    branch_proj = noise(seeds[4], (D, RNN_WIDTH), D ** -0.5, 0.125, ((0, 32),))
    output_proj = noise(seeds[5], (RNN_WIDTH, D), (RNN_WIDTH // 8) ** -0.5, 0.3125, ((0, 32),))
    recur_gate = noise(seeds[6], (RNN_WIDTH, HB), HB ** -0.5, 0.375, ((0, 32),))
    inlet_gate = noise(seeds[7], (RNN_WIDTH, HB), HB ** -0.5, 0.375, ((0, 32),))
    conv_kernel = noise(seeds[8], (4, RNN_WIDTH), 0.5, 3.0, ((1, 32),))
    conv_bias = noise(seeds[9], (RNN_WIDTH,), 0.5, 3.0, ((0, 32),))
    recur_bias = noise(seeds[10], (RNN_WIDTH,), 1.0, 4.0, ((0, 32),))
    inlet_bias = noise(seeds[11], (RNN_WIDTH,), 1.0, 4.0, ((0, 32),))
    decay_param = draw_decay_param(jax.random.fold_in(seeds[18], 71), 0)
    mixer_gain = jnp.clip(1.0 + 0.1 * jax.random.normal(seeds[13], (D,), jnp.float32), 0.5, 1.5).astype(jnp.bfloat16)
    feed_gain = jnp.clip(1.0 + 0.1 * jax.random.normal(seeds[14], (D,), jnp.float32), 0.5, 1.5).astype(jnp.bfloat16)
    feed_gate = noise(seeds[15], (D, FF), D ** -0.5, 0.125, ((0, 8), (1, 4)))
    feed_up = noise(seeds[16], (D, FF), D ** -0.5, 0.125, ((0, 8), (1, 4)))
    feed_down = noise(seeds[17], (FF, D), FF ** -0.5, 0.078125, ((0, 4), (1, 8)))
    return dict(tokens=tokens, lengths=lengths, cotangent=cotangent, input_proj=input_proj, branch_proj=branch_proj, output_proj=output_proj, recur_gate=recur_gate, inlet_gate=inlet_gate, conv_kernel=conv_kernel, conv_bias=conv_bias, recur_bias=recur_bias, inlet_bias=inlet_bias, decay_param=decay_param, mixer_gain=mixer_gain, feed_gain=feed_gain, feed_gate=feed_gate, feed_up=feed_up, feed_down=feed_down)


@jax.custom_vjp
def low(v):
    return lax.optimization_barrier(v.astype(jnp.bfloat16)).astype(jnp.float32)

@jax.custom_vjp
def low_back(v):
    return v

def low_keep(v):
    return (low(v), None)

def low_pass(kept, grad):
    return (grad,)

def back_keep(v):
    return (v, None)

def back_low(kept, grad):
    return (low(grad),)
low.defvjp(low_keep, low_pass)
low_back.defvjp(back_keep, back_low)
highest = lax.Precision.HIGHEST
epsilon = 1e-06

def product(left, right):
    return jnp.dot(left, right, precision=highest)

def rms_scaled(values, gain):
    return values * lax.rsqrt(lax.optimization_barrier(jnp.mean(values * values, axis=-1, keepdims=True)) + epsilon) * gain

def affine_join(earlier, later):
    return (earlier[0] * later[0], later[0] * earlier[1] + later[1])

def block_forward(validity, tokens, input_proj, branch_proj, output_proj, recur_gate, inlet_gate, conv_kernel, conv_bias, recur_bias, inlet_bias, decay_param, mixer_gain, feed_gain, feed_gate, feed_up, feed_down):
    length = tokens.shape[0]
    normed = low(rms_scaled(tokens, mixer_gain))
    branch = low_back(product(normed, branch_proj))
    gate_values = jax.nn.gelu(branch, approximate=True)
    inner_proj = low(low_back(product(normed, input_proj)))
    padded = jnp.concatenate([jnp.zeros((3, inner_proj.shape[1]), jnp.float32), inner_proj], axis=0)
    convolved = conv_bias + conv_kernel[0] * padded[3:3 + length]
    for offset in range(1, 4):
        convolved = convolved + conv_kernel[offset] * padded[3 - offset:3 - offset + length]
    convolved = low(convolved)
    head_view = convolved.reshape(length, NH, HB)
    recur_pre = low_back(jnp.einsum('thi,hij->thj', head_view, recur_gate.reshape(NH, HB, HB), precision=highest)).reshape(length, NH * HB) + recur_bias
    inlet_pre = low_back(jnp.einsum('thi,hij->thj', head_view, inlet_gate.reshape(NH, HB, HB), precision=highest)).reshape(length, NH * HB) + inlet_bias
    recurrence = jax.nn.sigmoid(recur_pre)
    inlets = jax.nn.sigmoid(inlet_pre)
    log_decay = -8.0 * recurrence * jax.nn.softplus(decay_param)
    decays = jnp.exp(log_decay)
    scaling = jnp.sqrt(-jnp.expm1(2.0 * log_decay))
    cumulative, states = lax.associative_scan(affine_join, (decays, scaling * inlets * convolved), axis=0)
    mixed_in = low(gate_values * states)
    mix = low_back(product(mixed_in, output_proj))
    middle = tokens + validity * mix
    normed_two = low(rms_scaled(middle, feed_gain))
    feed_pre = low_back(product(normed_two, feed_gate))
    feed_lin = low_back(product(normed_two, feed_up))
    hidden = low(jax.nn.gelu(feed_pre, approximate=True) * feed_lin)
    feed_out = low_back(product(hidden, feed_down))
    return middle + validity * feed_out

def reference(tokens, lengths, cotangent, input_proj, branch_proj, output_proj, recur_gate, inlet_gate, conv_kernel, conv_bias, recur_bias, inlet_bias, decay_param, mixer_gain, feed_gain, feed_gate, feed_up, feed_down):
    weights = tuple((entry.astype(jnp.float32) for entry in (input_proj, branch_proj, output_proj, recur_gate, inlet_gate, conv_kernel, conv_bias, recur_bias, inlet_bias, decay_param, mixer_gain, feed_gain, feed_gate, feed_up, feed_down)))
    positions = jnp.arange(LENGTH, dtype=jnp.int32)

    def per_sequence(running, item):
        sequence, length, grad_out = item
        validity = (positions < length.astype(jnp.int32)).astype(jnp.float32)[:, None]
        result, pull = jax.vjp(partial(block_forward, validity), sequence.astype(jnp.float32), *weights)
        grads = pull(grad_out.astype(jnp.float32))
        updated = tuple((earlier + update for earlier, update in zip(running, grads[1:])))
        return (updated, (result.astype(jnp.bfloat16), grads[0]))
    start_sums = tuple((jnp.zeros_like(entry) for entry in weights))
    totals, stacked = lax.scan(per_sequence, start_sums, (tokens, lengths, cotangent))
    return (stacked[0], stacked[1], totals[0], totals[1], totals[2], totals[3], totals[4], totals[5], totals[6], totals[7], totals[8], totals[9], totals[10], totals[11], totals[12], totals[13], totals[14])
```

```python
import functools

import jax
import jax.numpy as jnp
from jax import lax
from jax.experimental import pallas as pl
from jax.experimental.pallas import tpu as pltpu
from jax.sharding import Mesh
from jax.sharding import PartitionSpec as P

HB = 256
EVERY = ("x", "core", "z", "y")
F32 = jnp.float32
BF16 = jnp.bfloat16

epsilon = 1e-06


def rotated(block, axis, distance):
    count = lax.axis_size(axis)
    return lax.ppermute(block, axis, [(i, (i + distance) % count) for i in range(count)])


def shifted(block, axis, distance):
    count = lax.axis_size(axis)
    route = [(i, i + distance) for i in range(count) if 0 <= i + distance < count]
    return lax.ppermute(block, axis, route)


def spread(block, axis, dim):
    count = lax.axis_size(axis)
    place = lax.axis_index(axis)
    if count == 2:
        other = rotated(block, axis, 1)
        low = place == 0
        return jnp.stack(
            [jnp.where(low, block, other), jnp.where(low, other, block)], axis=dim
        )
    shape = block.shape[:dim] + (count,) + block.shape[dim:]
    whole = jnp.zeros(shape, block.dtype)
    for distance in range(count):
        piece = block if distance == 0 else rotated(block, axis, distance)
        source = lax.rem(place - distance + count, count)
        whole = lax.dynamic_update_slice_in_dim(
            whole, jnp.expand_dims(piece, dim), source, dim
        )
    return whole


def pick(array, index, dim):
    return lax.dynamic_index_in_dim(array, index, dim, keepdims=False)


def collect(partial, axis, dim):
    count = lax.axis_size(axis)
    place = lax.axis_index(axis)
    if count == 2:
        got = rotated(pick(partial, 1 - place, dim).astype(BF16), axis, 1)
        return pick(partial, place, dim).astype(F32) + got.astype(F32)
    blocks = jnp.moveaxis(partial, dim, 0).astype(BF16)
    got = lax.all_to_all(blocks, axis, 0, 0)
    return jnp.sum(got.astype(F32), axis=0)


def pair_rows(block):
    return spread(block, "core", 0).reshape((2 * block.shape[0],) + block.shape[1:])


def pair_sum(partial):
    rows = partial.shape[0] // 2
    halves = partial.reshape(2, rows, partial.shape[1])
    core = lax.axis_index("core")
    return pick(halves, core, 0) + rotated(pick(halves, 1 - core, 0), "core", 1)


def swap_columns(block):
    rows, width = block.shape[0], block.shape[1] // 2
    halves = block.reshape(rows, 2, width)
    core = lax.axis_index("core")
    own = pick(halves, core, 1)
    other = rotated(pick(halves, 1 - core, 1), "core", 1)
    low = core == 0
    return jnp.stack([jnp.where(low, own, other), jnp.where(low, other, own)], axis=0)


def unswap_columns(rows_both):
    core = lax.axis_index("core")
    own = pick(rows_both, core, 0)
    other = rotated(pick(rows_both, 1 - core, 0), "core", 1)
    low = core == 0
    return jnp.concatenate([jnp.where(low, own, other), jnp.where(low, other, own)], axis=1)


def half_route():
    count = lax.axis_size("x")
    return [(s, (s % count) * 2 + s // count) for s in range(2 * count)]


def to_half(block):
    return lax.ppermute(block, ("x", "core"), half_route())


def from_half(block):
    return lax.ppermute(block, ("x", "core"), [(b, a) for a, b in half_route()])


def share_small(vector):
    count = lax.axis_size(EVERY)
    return lax.all_to_all(jnp.broadcast_to(vector[None], (count,) + vector.shape), EVERY, 0, 0)


def gelu_tanh(values):
    return jax.nn.gelu(values, approximate=True)


def rms_factor(values):
    return lax.rsqrt(jnp.mean(values * values, axis=-1, keepdims=True) + epsilon)


def norm_backward(grad_normed, scaled, factor, gain):
    weighted = grad_normed * gain
    inner_mean = jnp.mean(weighted * scaled, axis=-1, keepdims=True)
    return (factor * (weighted - scaled * inner_mean), jnp.sum(grad_normed * scaled, axis=0))


def scan_kernel(reverse, decay_ref, drive_ref, cumulative_ref, local_ref):
    decay, drive = decay_ref[...], drive_ref[...]
    rows, width = decay.shape
    step = 1
    while step < rows:
        ones, zeros = jnp.ones((step, width), F32), jnp.zeros((step, width), F32)
        if reverse:
            decay_before = jnp.concatenate([decay[step:], ones], axis=0)
            drive_before = jnp.concatenate([drive[step:], zeros], axis=0)
        else:
            decay_before = jnp.concatenate([ones, decay[: rows - step]], axis=0)
            drive_before = jnp.concatenate([zeros, drive[: rows - step]], axis=0)
        drive = drive + decay * drive_before
        decay = decay * decay_before
        step *= 2
    cumulative_ref[...] = decay
    local_ref[...] = drive


def scan(decay, drive, reverse):
    rows, width = decay.shape
    block = pl.BlockSpec((rows, HB), lambda i: (0, i))
    shape = jax.ShapeDtypeStruct((rows, width), F32)
    return pl.pallas_call(
        functools.partial(scan_kernel, reverse),
        grid=(width // HB,),
        in_specs=[block, block],
        out_specs=[block, block],
        out_shape=[shape, shape],
        compiler_params=pltpu.CompilerParams(vmem_limit_bytes=32 << 20),
        cost_estimate=pl.CostEstimate(
            flops=24 * rows * width, bytes_accessed=16 * rows * width, transcendentals=0
        ),
    )(decay, drive)


def head_product(values, weights):
    rows, width = values.shape
    heads = width // HB
    return jnp.einsum(
        "thi,hij->thj",
        values.reshape(rows, heads, HB),
        weights.reshape(heads, HB, HB),
        preferred_element_type=F32,
    ).reshape(rows, width)


def head_product_back(values, weights):
    rows, width = values.shape
    heads = width // HB
    return jnp.einsum(
        "thj,hij->thi",
        values.reshape(rows, heads, HB),
        weights.reshape(heads, HB, HB),
        preferred_element_type=F32,
    ).reshape(rows, width)


def head_outer(left, right):
    rows, width = left.shape
    heads = width // HB
    return jnp.einsum(
        "thi,thj->hij",
        left.reshape(rows, heads, HB),
        right.reshape(rows, heads, HB),
        preferred_element_type=F32,
    ).reshape(width, HB)


def dot(left, right):
    return jnp.dot(left, right, preferred_element_type=F32)


def dot_t(left, right):
    return lax.dot_general(left, right, (((1,), (1,)), ((), ())), preferred_element_type=F32)


def outer(left, right):
    return lax.dot_general(left, right, (((0,), (0,)), ((), ())), preferred_element_type=F32)


def gather_rows(block):
    rows, width = block.shape[1:]
    block = spread(block, "z", 1)
    block = spread(block, "y", 2)
    block = spread(block, "x", 0)
    return block.reshape(-1, width)


def gather_half(block):
    width = block.shape[1]
    block = spread(block, "z", 0)
    block = spread(block, "y", 1)
    block = spread(block, "x", 0)
    return block.reshape(-1, width)


def gather_feed(block):
    width = block.shape[1]
    block = spread(block, "z", 0)
    block = spread(block, "y", 1)
    return block.reshape(-1, width)


def sum_rows(left, right, rows):
    x_count, z_count, y_count = (lax.axis_size(a) for a in ("x", "z", "y"))
    width = right.shape[1]
    partial = outer(left, right).reshape(x_count, 2, z_count, y_count, rows, width)
    partial = collect(partial, "x", 0)
    partial = collect(partial, "y", 2)
    return collect(partial, "z", 1)


def sum_half(partial, rows):
    x_count, z_count, y_count = (lax.axis_size(a) for a in ("x", "z", "y"))
    width = partial.shape[1]
    partial = partial.reshape(x_count, z_count, y_count, rows, width)
    partial = collect(partial, "x", 0)
    partial = collect(partial, "y", 1)
    return from_half(collect(partial, "z", 0).astype(BF16)).astype(F32)


def sum_feed(left, right):
    z_count, y_count = lax.axis_size("z"), lax.axis_size("y")
    rows, width = left.shape[1] // (z_count * y_count), right.shape[1]
    place = lax.axis_index("y")
    columns = left.reshape(left.shape[0], z_count, y_count, rows)

    def part(which):
        return outer(pick(columns, which, 2).reshape(left.shape[0], z_count * rows), right)

    got = rotated(part(1 - place).astype(BF16), "y", 1)
    total = part(place) + got.astype(F32)
    return collect(total.reshape(z_count, rows, width), "z", 0)


def on_device(
    tokens,
    lengths,
    cotangent,
    input_proj,
    branch_proj,
    output_proj,
    recur_gate,
    inlet_gate,
    conv_kernel,
    conv_bias,
    recur_bias,
    inlet_bias,
    decay_param,
    mixer_gain,
    feed_gain,
    feed_gate,
    feed_up,
    feed_down,
):
    x_count, z_count, y_count = (lax.axis_size(a) for a in ("x", "z", "y"))
    x_place, core = lax.axis_index("x"), lax.axis_index("core")
    own_rows, model = tokens.shape[1:]
    channels = conv_kernel.shape[1]
    gain_width = mixer_gain.shape[0]
    first = (x_place * 2 + core) * own_rows
    positions = first + jnp.arange(own_rows, dtype=jnp.int32)
    validity = (positions < lengths[0]).astype(F32)[:, None]

    vectors = jnp.concatenate(
        [
            conv_kernel.reshape(-1),
            conv_bias,
            recur_bias,
            inlet_bias,
            decay_param,
            mixer_gain,
            feed_gain,
        ]
    )
    everyone = share_small(vectors)
    by_channel = everyone[:, : 8 * channels].reshape(-1, 8, channels)
    gains = everyone[:, 8 * channels :].reshape(-1, 2, gain_width).transpose(1, 0, 2)
    gain_one, gain_two = gains.reshape(2, -1).astype(F32)
    half = by_channel.shape[0] // 2
    by_channel = lax.dynamic_slice_in_dim(by_channel, core * half, half, 0)
    by_channel = by_channel.transpose(1, 0, 2).reshape(8, -1).astype(F32)
    kernel_wide, bias_conv, bias_recur, bias_inlet, param_wide = (
        by_channel[:4],
        by_channel[4],
        by_channel[5],
        by_channel[6],
        by_channel[7],
    )

    input_full = gather_rows(swap_columns(input_proj))
    branch_full = gather_rows(swap_columns(branch_proj))
    gates_full = gather_half(to_half(jnp.concatenate([recur_gate, inlet_gate], axis=1)))
    recur_full, inlet_full = gates_full[:, :HB], gates_full[:, HB:]
    output_full = gather_half(to_half(output_proj))
    gate_local = gather_feed(feed_gate)
    lin_local = gather_feed(feed_up)
    down_local = gather_feed(feed_down.T)

    grad_out = cotangent[0].astype(F32)
    grad_feed = (validity * grad_out).astype(BF16)
    everyones_rows = lambda block: spread(spread(block, "x", 0), "core", 1).reshape(-1, model)
    grad_all = everyones_rows(grad_feed)

    channel_rate = jax.nn.softplus(param_wide)
    token_rows = tokens[0].astype(F32)
    factor_one = rms_factor(token_rows)
    scaled_one = token_rows * factor_one
    normed = pair_rows((scaled_one * gain_one).astype(BF16))
    rows = normed.shape[0]
    branch = dot(normed, branch_full)
    inner_proj = dot(normed, input_full).astype(BF16)
    rim_rows = shifted(inner_proj[rows - 3 :], "x", 1)
    extended = jnp.concatenate([rim_rows, inner_proj], axis=0)
    extended_wide = extended.astype(F32)
    convolved = bias_conv + kernel_wide[0] * extended_wide[3 : 3 + rows]
    for offset in range(1, 4):
        convolved = convolved + kernel_wide[offset] * extended_wide[3 - offset : 3 - offset + rows]
    conv_low = convolved.astype(BF16)
    recurrence = jax.nn.sigmoid(head_product(conv_low, recur_full) + bias_recur)
    inlets = jax.nn.sigmoid(head_product(conv_low, inlet_full) + bias_inlet)
    log_decay = -8.0 * recurrence * channel_rate
    decays = jnp.exp(log_decay)
    scaling = jnp.sqrt(-jnp.expm1(2.0 * log_decay))
    conv_value = conv_low.astype(F32)
    cumulative, local_state = scan(decays, scaling * inlets * conv_value, False)
    state_in = jnp.zeros_like(local_state[0])
    for _ in range(x_count - 1):
        state_in = shifted(cumulative[rows - 1] * state_in + local_state[rows - 1], "x", 1)
    states = local_state + cumulative * state_in
    gate_values = gelu_tanh(branch)
    mixed_in = (gate_values * states).astype(BF16)
    mix = pair_sum(dot(mixed_in, output_full))
    middle = token_rows + validity * mix
    factor_two = rms_factor(middle)
    scaled_two = middle * factor_two
    normed_two = (scaled_two * gain_two).astype(BF16)

    all_rows = everyones_rows(normed_two)
    feed_pre = dot(all_rows, gate_local)
    feed_lin = dot(all_rows, lin_local)
    feed_act, gelu_pull = jax.vjp(gelu_tanh, feed_pre)
    hidden = (feed_act * feed_lin).astype(BF16)
    feed_grad_down = sum_feed(grad_all, hidden).T
    grad_hidden = dot(grad_all, down_local)
    grad_pre = gelu_pull(grad_hidden * feed_lin)[0].astype(BF16)
    grad_lin = (grad_hidden * feed_act).astype(BF16)
    grad_rows = dot_t(grad_pre, gate_local) + dot_t(grad_lin, lin_local)

    def owners_rows(partial):
        block = partial.reshape(x_count, 2, own_rows, model)
        block = pick(block, core, 1) + rotated(pick(block, 1 - core, 1), "core", 1)
        return collect(block, "x", 0)

    grad_normed_two = owners_rows(grad_rows)
    feed_out = owners_rows(dot_t(hidden, down_local))
    output = (middle + validity * feed_out).astype(BF16)[None]
    feed_grad_gate = sum_feed(all_rows, grad_pre)
    feed_grad_up = sum_feed(all_rows, grad_lin)

    grad_mid_norm, grad_gain_feed = norm_backward(grad_normed_two, scaled_two, factor_two, gain_two)
    grad_middle = grad_out + grad_mid_norm
    grad_mix = pair_rows((validity * grad_middle).astype(BF16))
    grad_output = sum_half(outer(mixed_in, grad_mix), output_proj.shape[0])
    grad_mixed = dot_t(grad_mix, output_full)
    grad_branch = jax.vjp(gelu_tanh, branch)[1](grad_mixed * states)[0].astype(BF16)
    grad_branch_proj = unswap_columns(sum_rows(normed, grad_branch, branch_proj.shape[0]))
    grad_states = grad_mixed * gate_values
    next_decays = jnp.concatenate([decays[1:], jnp.ones_like(decays[:1])], axis=0)
    back_cum, back_local = scan(next_decays, grad_states, True)
    incoming = jnp.zeros_like(back_local[0])
    for _ in range(x_count - 1):
        incoming = shifted(decays[0] * (back_cum[0] * incoming + back_local[0]), "x", -1)
    carried = back_local + back_cum * incoming
    previous = jnp.concatenate([state_in[None], states[:-1]], axis=0)
    drive_grad = carried * conv_value
    grad_log = carried * previous * decays - drive_grad * inlets * decays * decays / scaling
    grad_recur_pre = grad_log * (-8.0 * channel_rate) * recurrence * (1.0 - recurrence)
    grad_inlet_pre = drive_grad * scaling * inlets * (1.0 - inlets)
    grad_param = jnp.sum(grad_log * (-8.0 * recurrence), axis=0) * jax.nn.sigmoid(param_wide)
    rounded_recur = grad_recur_pre.astype(BF16)
    rounded_inlet = grad_inlet_pre.astype(BF16)
    grad_gates = sum_half(
        jnp.concatenate(
            [head_outer(conv_low, rounded_recur), head_outer(conv_low, rounded_inlet)], axis=1
        ),
        channels,
    )
    grad_conv = (
        carried * scaling * inlets
        + head_product_back(rounded_recur, recur_full)
        + head_product_back(rounded_inlet, inlet_full)
    )
    ahead = shifted(grad_conv[:3], "x", -1)
    extended_back = jnp.concatenate([grad_conv, ahead], axis=0)
    grad_inner = kernel_wide[0] * extended_back[0:rows]
    for offset in range(1, 4):
        grad_inner = grad_inner + kernel_wide[offset] * extended_back[offset : offset + rows]
    grad_inner = grad_inner.astype(BF16)
    grad_input_proj = unswap_columns(sum_rows(normed, grad_inner, input_proj.shape[0]))
    grad_kernel = jnp.stack(
        [
            jnp.sum(grad_conv * extended_wide[3 - offset : 3 - offset + rows], axis=0)
            for offset in range(4)
        ],
        axis=0,
    )
    grad_normed = pair_sum(dot_t(grad_inner, input_full) + dot_t(grad_branch, branch_full))
    grad_token_norm, grad_gain_mixer = norm_backward(grad_normed, scaled_one, factor_one, gain_one)
    grad_tokens = (grad_middle + grad_token_norm)[None]

    channel_sums = jnp.concatenate(
        [
            grad_kernel,
            jnp.stack(
                [
                    jnp.sum(grad_conv, axis=0),
                    jnp.sum(grad_recur_pre, axis=0),
                    jnp.sum(grad_inlet_pre, axis=0),
                    grad_param,
                ]
            ),
        ],
        axis=0,
    )
    channel_sums = channel_sums.reshape(8, half, channels).transpose(1, 0, 2)
    everyones = lax.dynamic_update_slice_in_dim(
        jnp.zeros((2 * half, 8, channels), F32), channel_sums, core * half, 0
    ).reshape(2 * half, 8 * channels)
    gain_sums = jnp.stack([grad_gain_mixer, grad_gain_feed]).reshape(2, 2 * half, gain_width)
    everyones = jnp.concatenate(
        [everyones, gain_sums.transpose(1, 0, 2).reshape(2 * half, 2 * gain_width)], axis=1
    )
    sums = jnp.sum(lax.all_to_all(everyones, EVERY, 0, 0), axis=0)
    by_channel = sums[: 8 * channels].reshape(8, channels)
    by_gain = sums[8 * channels :].reshape(2, gain_width)
    return (
        output,
        grad_tokens,
        grad_input_proj,
        grad_branch_proj,
        grad_output,
        grad_gates[:, :HB],
        grad_gates[:, HB:],
        by_channel[:4],
        by_channel[4],
        by_channel[5],
        by_channel[6],
        by_channel[7],
        by_gain[0],
        by_gain[1],
        feed_grad_gate,
        feed_grad_up,
        feed_grad_down,
    )


def solution(mesh):
    seq, batch = mesh.shape["seq"], mesh.shape["batch"]
    fine = Mesh(mesh.devices.reshape(seq // 2, 2, batch // 2, 2), EVERY)
    sequences, places = ("z", "y"), ("x", "core")
    rows = P(sequences, places, None)
    spread_rows, spread_columns, spread_all = P(EVERY, None), P(None, EVERY), P(EVERY)
    feed = P(sequences, places)
    feed_back = P(places, sequences)
    in_specs = (
        (rows, P(sequences), rows)
        + (spread_rows,) * 5
        + (spread_columns,)
        + (spread_all,) * 6
        + (feed, feed, feed_back)
    )
    out_specs = (
        (rows, rows)
        + (spread_rows,) * 5
        + (spread_columns,)
        + (spread_all,) * 6
        + (feed, feed, feed_back)
    )
    return jax.shard_map(
        on_device, mesh=fine, in_specs=in_specs, out_specs=out_specs, check_vma=False
    )
```

```python
import functools

import jax
import jax.numpy as jnp
from jax import lax
from jax.experimental import pallas as pl
from jax.experimental.pallas import tpu as pltpu
from jax.sharding import Mesh
from jax.sharding import PartitionSpec as P

HB = 256
EVERY = ("x", "core", "zh", "zl", "y")
F32 = jnp.float32
BF16 = jnp.bfloat16

epsilon = 1e-06


def rotated(block, axis, distance):
    count = lax.axis_size(axis)
    return lax.ppermute(block, axis, [(i, (i + distance) % count) for i in range(count)])


def shifted(block, axis, distance):
    count = lax.axis_size(axis)
    route = [(i, i + distance) for i in range(count) if 0 <= i + distance < count]
    return lax.ppermute(block, axis, route)


def after(value, *earlier):
    return lax.optimization_barrier((value,) + earlier)[0]


def pick(array, index, dim):
    return lax.dynamic_index_in_dim(array, index, dim, keepdims=False)


def received(block, axis):
    return [block] + [rotated(block, axis, d) for d in range(1, lax.axis_size(axis))]


def spread_near(block, axis, dim):
    return jnp.stack(received(block, axis), axis=dim)


def near(array, axis, dim):
    count = lax.axis_size(axis)
    place = lax.axis_index(axis)
    if count == 2:
        return jnp.where(place == 0, array, jnp.flip(array, dim))
    return jnp.stack(
        [pick(array, lax.rem(place - d + count, count), dim) for d in range(count)], axis=dim
    )


def spread(block, axis, dim):
    count = lax.axis_size(axis)
    place = lax.axis_index(axis)
    pieces = received(block, axis)
    if count == 2:
        low = place == 0
        return jnp.stack(
            [jnp.where(low, pieces[0], pieces[1]), jnp.where(low, pieces[1], pieces[0])], axis=dim
        )
    shape = block.shape[:dim] + (count,) + block.shape[dim:]
    whole = jnp.zeros(shape, block.dtype)
    for d, piece in enumerate(pieces):
        source = lax.rem(place - d + count, count)
        whole = lax.dynamic_update_slice_in_dim(whole, jnp.expand_dims(piece, dim), source, dim)
    return whole


def collect_near(part, axis):
    count = lax.axis_size(axis)
    got = [rotated(part(d).astype(BF16), axis, count - d) for d in range(1, count)]
    return sum([g.astype(F32) for g in got], part(0).astype(F32))


def collect_dim(partial, axis, dim):
    return collect_near(lambda d: lax.index_in_dim(partial, d, dim, keepdims=False), axis)


def collect(partial, axis, dim):
    count = lax.axis_size(axis)
    place = lax.axis_index(axis)
    return collect_near(lambda d: pick(partial, lax.rem(place - d + count, count), dim), axis)


def pair_rows(block):
    return spread(block, "core", 0).reshape((2 * block.shape[0],) + block.shape[1:])


def pair_sum(partial):
    rows = partial.shape[0] // 2
    halves = partial.reshape(2, rows, partial.shape[1])
    core = lax.axis_index("core")
    return pick(halves, core, 0) + rotated(pick(halves, 1 - core, 0), "core", 1)


def swap_columns(block):
    rows, width = block.shape[0], block.shape[1] // 2
    halves = block.reshape(rows, 2, width)
    core = lax.axis_index("core")
    own = pick(halves, core, 1)
    other = rotated(pick(halves, 1 - core, 1), "core", 1)
    low = core == 0
    return jnp.stack([jnp.where(low, own, other), jnp.where(low, other, own)], axis=0)


def unswap_columns(rows_both):
    core = lax.axis_index("core")
    own = pick(rows_both, core, 0)
    other = rotated(pick(rows_both, 1 - core, 0), "core", 1)
    low = core == 0
    return jnp.concatenate([jnp.where(low, own, other), jnp.where(low, other, own)], axis=1)


def half_route():
    count = lax.axis_size("x")
    return [(s, (s % count) * 2 + s // count) for s in range(2 * count)]


def to_half(block):
    return lax.ppermute(block, ("x", "core"), half_route())


def from_half(block):
    return lax.ppermute(block, ("x", "core"), [(b, a) for a, b in half_route()])


def share_small(vector):
    count = lax.axis_size(EVERY)
    return lax.all_to_all(jnp.broadcast_to(vector[None], (count,) + vector.shape), EVERY, 0, 0)


def gelu_tanh(values):
    return jax.nn.gelu(values, approximate=True)


def rms_factor(values):
    return lax.rsqrt(jnp.mean(values * values, axis=-1, keepdims=True) + epsilon)


def norm_backward(grad_normed, scaled, factor, gain):
    weighted = grad_normed * gain
    inner_mean = jnp.mean(weighted * scaled, axis=-1, keepdims=True)
    return (factor * (weighted - scaled * inner_mean), jnp.sum(grad_normed * scaled, axis=0))


def scan_kernel(reverse, decay_ref, drive_ref, cumulative_ref, local_ref):
    decay, drive = decay_ref[...], drive_ref[...]
    rows, width = decay.shape
    step = 1
    while step < rows:
        ones, zeros = jnp.ones((step, width), F32), jnp.zeros((step, width), F32)
        if reverse:
            decay_before = jnp.concatenate([decay[step:], ones], axis=0)
            drive_before = jnp.concatenate([drive[step:], zeros], axis=0)
        else:
            decay_before = jnp.concatenate([ones, decay[: rows - step]], axis=0)
            drive_before = jnp.concatenate([zeros, drive[: rows - step]], axis=0)
        drive = drive + decay * drive_before
        decay = decay * decay_before
        step *= 2
    cumulative_ref[...] = decay
    local_ref[...] = drive


def scan(decay, drive, reverse):
    rows, width = decay.shape
    block = pl.BlockSpec((rows, HB), lambda i: (0, i))
    shape = jax.ShapeDtypeStruct((rows, width), F32)
    return pl.pallas_call(
        functools.partial(scan_kernel, reverse),
        grid=(width // HB,),
        in_specs=[block, block],
        out_specs=[block, block],
        out_shape=[shape, shape],
        compiler_params=pltpu.CompilerParams(vmem_limit_bytes=32 << 20),
        cost_estimate=pl.CostEstimate(
            flops=24 * rows * width, bytes_accessed=16 * rows * width, transcendentals=0
        ),
    )(decay, drive)


def head_product(values, weights):
    rows, width = values.shape
    heads = width // HB
    return jnp.einsum(
        "thi,hij->thj",
        values.reshape(rows, heads, HB),
        weights.reshape(heads, HB, HB),
        preferred_element_type=F32,
    ).reshape(rows, width)


def head_product_back(values, weights):
    rows, width = values.shape
    heads = width // HB
    return jnp.einsum(
        "thj,hij->thi",
        values.reshape(rows, heads, HB),
        weights.reshape(heads, HB, HB),
        preferred_element_type=F32,
    ).reshape(rows, width)


def head_outer(left, right):
    rows, width = left.shape
    heads = width // HB
    return jnp.einsum(
        "thi,thj->hij",
        left.reshape(rows, heads, HB),
        right.reshape(rows, heads, HB),
        preferred_element_type=F32,
    ).reshape(width, HB)


def dot(left, right):
    return jnp.dot(left, right, preferred_element_type=F32)


def dot_t(left, right):
    return lax.dot_general(left, right, (((1,), (1,)), ((), ())), preferred_element_type=F32)


def outer(left, right):
    return lax.dot_general(left, right, (((0,), (0,)), ((), ())), preferred_element_type=F32)


def sizes(*axes):
    return tuple(lax.axis_size(axis) for axis in axes)


def flat(block):
    return block.reshape(-1, block.shape[-1])


def mixer_order(values):
    rows = values.shape[0]
    values = values.reshape((rows,) + sizes(*EVERY) + (-1,))
    for axis, dim in (("x", 1), ("zh", 3), ("zl", 4), ("y", 5)):
        values = near(values, axis, dim)
    return values.transpose(0, 2, 1, 5, 4, 3, 6).reshape(rows, -1)


def mixer_order_back(values):
    rows = values.shape[0]
    values = values.reshape((rows,) + sizes("core", "x", "y", "zl", "zh") + (-1,))
    values = values.transpose(0, 2, 1, 5, 4, 3, 6)
    for axis, dim in (("x", 1), ("zh", 3), ("zl", 4), ("y", 5)):
        values = near(values, axis, dim)
    return values.reshape(rows, -1)


def gather_rows(block, mark):
    width = block.shape[2]
    block = block if mark is None else after(block, mark)
    pieces = received(block, "zh")
    block = spread_near(jnp.stack(pieces, axis=1), "zl", 1)
    one = spread_near(spread_near(block[0], "y", 0), "x", 0)
    two = spread_near(spread_near(block[1], "x", 0), "y", 1)
    return jnp.concatenate([one.reshape(-1, width), two.reshape(-1, width)], axis=0), pieces[1]


def sum_rows(left, right, rows):
    x_count, y_count, l_count, h_count = sizes("x", "y", "zl", "zh")
    batch_rows = l_count * h_count * rows
    parts = left.shape[0], 2, x_count, y_count, batch_rows

    def part(c, x, y):
        start = ((c * x_count + x) * y_count + y) * batch_rows
        return left[:, start : start + batch_rows]

    def first_x(x):
        start = x * y_count * batch_rows
        return outer(left[:, start : start + y_count * batch_rows], right)

    def first_y(y):
        return jnp.concatenate([outer(part(1, x, y), right) for x in range(x_count)], axis=0)

    one = collect_near(first_x, "x").reshape(y_count, l_count, h_count, rows, -1)
    two = collect_near(first_y, "y").reshape(x_count, l_count, h_count, rows, -1)
    both = jnp.stack([collect_dim(one, "y", 0), collect_dim(two, "x", 0)], axis=2)
    return collect_dim(collect_dim(both, "zl", 0), "zh", 0)


def along_batch(block, mark):
    pieces = after(block, mark)
    block = spread(pieces, "zh", 0)
    arrived = block
    return spread(spread(block, "zl", 1), "y", 2), arrived


def pieces_of_x(block):
    count = lax.axis_size("x")
    place = lax.axis_index("x")
    return [
        (flat(piece), lax.rem(place - d + count, count))
        for d, piece in enumerate(received(block, "x"))
    ]


def columns_of(values, place, width):
    return lax.dynamic_slice_in_dim(values, place * width, width, 1)


def times_pieces(values, pieces):
    width = pieces[0][0].shape[0]
    return sum(dot(columns_of(values, place, width), piece) for piece, place in pieces)


def times_pieces_t(values, pieces):
    parts = jnp.stack([dot_t(values, piece) for piece, place in pieces], axis=1)
    return near(parts, "x", 1).reshape(values.shape[0], -1)


def sum_half(part, rows):
    h_count, l_count, y_count = sizes("zh", "zl", "y")
    count = lax.axis_size("x")
    place = lax.axis_index("x")
    partial = collect_near(lambda d: part(lax.rem(place - d + count, count)), "x")
    partial = partial.reshape(h_count, l_count, y_count, rows, partial.shape[-1])
    partial = collect(partial, "y", 2)
    partial = collect(partial, "zl", 1)
    return from_half(collect(partial, "zh", 0).astype(BF16)).astype(F32)


def split_feed(block):
    rows, width = block.shape[0], block.shape[1] // 2
    halves = block.reshape(rows, 2, width)
    place = lax.axis_index("y")
    own = pick(halves, place, 1)
    other = rotated(pick(halves, 1 - place, 1), "y", 1)
    low = place == 0
    return jnp.stack([jnp.where(low, own, other), jnp.where(low, other, own)], axis=0)


def unsplit_feed(block):
    place = lax.axis_index("y")
    own = pick(block, place, 0)
    other = rotated(pick(block, 1 - place, 0).astype(BF16), "y", 1).astype(F32)
    low = place == 0
    return jnp.concatenate([jnp.where(low, own, other), jnp.where(low, other, own)], axis=1)


def gather_feed(block, mark):
    block = after(flat(block), mark)
    return lax.all_gather(block, ("zh", "zl"), axis=0, tiled=True)


def sum_feed(left, right):
    total = outer(left, right).astype(BF16)
    total = lax.psum_scatter(total, ("zh", "zl"), scatter_dimension=0, tiled=True)
    return unsplit_feed(total.reshape(2, -1, right.shape[1]).astype(F32))


def everyones_rows(block):
    middle = block.shape[0] // 2
    one = spread_near(spread_near(block[:middle], "x", 0), "y", 0)
    two = spread_near(spread_near(block[middle:], "y", 0), "x", 0)
    return flat(spread_near(jnp.concatenate([flat(one), flat(two)], axis=0), "core", 0))


def owners_rows(partial):
    x_count, y_count = sizes("x", "y")
    width = partial.shape[1]
    block = collect_dim(partial.reshape(2, -1, width), "core", 0)
    middle = block.shape[0] // 2
    one = block[:middle].reshape(y_count, x_count, -1, width)
    two = block[middle:].reshape(x_count, y_count, -1, width)
    one = collect_dim(collect_dim(one, "y", 0), "x", 0)
    two = collect_dim(collect_dim(two, "x", 0), "y", 0)
    return jnp.concatenate([one, two], axis=0)


def on_device(
    tokens,
    lengths,
    cotangent,
    input_proj,
    branch_proj,
    output_proj,
    recur_gate,
    inlet_gate,
    conv_kernel,
    conv_bias,
    recur_bias,
    inlet_bias,
    decay_param,
    mixer_gain,
    feed_gain,
    feed_gate,
    feed_up,
    feed_down,
):
    x_count = lax.axis_size("x")
    x_place, core = lax.axis_index("x"), lax.axis_index("core")
    own_rows, model = tokens.shape[1:]
    channels = conv_kernel.shape[1]
    gain_width = mixer_gain.shape[0]
    first = (x_place * 2 + core) * own_rows
    positions = first + jnp.arange(own_rows, dtype=jnp.int32)
    validity = (positions < lengths[0]).astype(F32)[:, None]

    vectors = jnp.concatenate(
        [
            conv_kernel.reshape(-1),
            conv_bias,
            recur_bias,
            inlet_bias,
            decay_param,
            mixer_gain,
            feed_gain,
        ]
    )
    everyone = share_small(vectors)
    by_channel = everyone[:, : 8 * channels].reshape(-1, 8, channels)
    gains = everyone[:, 8 * channels :].reshape(-1, 2, gain_width).transpose(1, 0, 2)
    gain_one, gain_two = gains.reshape(2, -1).astype(F32)
    half = by_channel.shape[0] // 2
    by_channel = lax.dynamic_slice_in_dim(by_channel, core * half, half, 0)
    by_channel = by_channel.transpose(1, 0, 2).reshape(8, -1).astype(F32)
    kernel_wide, bias_conv, bias_recur, bias_inlet, param_wide = (
        by_channel[:4],
        by_channel[4],
        by_channel[5],
        by_channel[6],
        by_channel[7],
    )

    channel_rate = jax.nn.softplus(param_wide)
    token_rows = tokens[0].astype(F32)
    factor_one = rms_factor(token_rows)
    scaled_one = token_rows * factor_one
    normed = pair_rows(mixer_order((scaled_one * gain_one).astype(BF16)))
    rows = normed.shape[0]
    rim_normed = shifted(normed[rows - 8 :], "x", 1).reshape(8, 2, x_count, -1)
    rim_normed = jnp.roll(rim_normed, 1, axis=2).reshape(8, model)
    extended_normed = jnp.concatenate([rim_normed, normed], axis=0)

    input_full, mark = gather_rows(swap_columns(input_proj), None)
    gates = to_half(jnp.concatenate([recur_gate, inlet_gate], axis=1))
    gates_full = lax.all_gather(gates, ("x", "zh", "zl", "y"), axis=0, tiled=True)
    recur_full, inlet_full = gates_full[:, :HB], gates_full[:, HB:]
    branch_full, mark = gather_rows(swap_columns(branch_proj), mark)
    output_rows, mark = along_batch(to_half(output_proj), mark)
    output_full = pieces_of_x(output_rows)
    gate_local = gather_feed(split_feed(feed_gate), mark)
    lin_local = gather_feed(split_feed(feed_up), mark)
    down_local = gather_feed(split_feed(feed_down.T), mark)

    grad_out = cotangent[0].astype(F32)
    grad_feed = (validity * grad_out).astype(BF16)
    grad_all = everyones_rows(grad_feed)

    branch = dot(normed, branch_full)
    extended_wide = dot(extended_normed, input_full)[5:].astype(BF16).astype(F32)
    convolved = bias_conv + kernel_wide[0] * extended_wide[3 : 3 + rows]
    for offset in range(1, 4):
        convolved = convolved + kernel_wide[offset] * extended_wide[3 - offset : 3 - offset + rows]
    conv_low = convolved.astype(BF16)
    recurrence = jax.nn.sigmoid(head_product(conv_low, recur_full) + bias_recur)
    inlets = jax.nn.sigmoid(head_product(conv_low, inlet_full) + bias_inlet)
    log_decay = -8.0 * recurrence * channel_rate
    decays = jnp.exp(log_decay)
    scaling = jnp.sqrt(-jnp.expm1(2.0 * log_decay))
    conv_value = conv_low.astype(F32)
    cumulative, local_state = scan(decays, scaling * inlets * conv_value, False)
    state_in = jnp.zeros_like(local_state[0])
    for _ in range(x_count - 1):
        state_in = shifted(cumulative[rows - 1] * state_in + local_state[rows - 1], "x", 1)
    states = local_state + cumulative * state_in
    gate_values = gelu_tanh(branch)
    mixed_in = (gate_values * states).astype(BF16)
    mix = pair_sum(times_pieces(mixed_in, output_full))
    middle = token_rows + validity * mix
    factor_two = rms_factor(middle)
    scaled_two = middle * factor_two
    normed_two = (scaled_two * gain_two).astype(BF16)

    all_rows = everyones_rows(normed_two)
    feed_pre = dot(all_rows, gate_local)
    feed_lin = dot(all_rows, lin_local)
    feed_act, gelu_pull = jax.vjp(gelu_tanh, feed_pre)
    hidden = (feed_act * feed_lin).astype(BF16)
    feed_grad_down = sum_feed(grad_all, hidden).T
    grad_hidden = dot(grad_all, down_local)
    grad_pre = gelu_pull(grad_hidden * feed_lin)[0].astype(BF16)
    grad_lin = (grad_hidden * feed_act).astype(BF16)
    grad_rows = dot_t(grad_pre, gate_local) + dot_t(grad_lin, lin_local)
    grad_normed_two = owners_rows(grad_rows)
    later_rows, grad_pre, grad_lin = lax.optimization_barrier(
        (all_rows, grad_pre, grad_lin, grad_rows)
    )[:3]
    feed_grad_gate = sum_feed(later_rows, grad_pre)
    feed_grad_up = sum_feed(later_rows, grad_lin)

    grad_mid_norm, grad_gain_feed = norm_backward(grad_normed_two, scaled_two, factor_two, gain_two)
    grad_middle = grad_out + grad_mid_norm
    grad_mix = pair_rows((validity * grad_middle).astype(BF16))
    per_x = mixed_in.shape[1] // x_count
    grad_output = sum_half(
        lambda place: outer(columns_of(mixed_in, place, per_x), grad_mix), output_proj.shape[0]
    )
    feed_out = owners_rows(dot_t(after(hidden, grad_mix), down_local))
    output = (middle + validity * feed_out).astype(BF16)[None]
    grad_mixed = times_pieces_t(grad_mix, output_full)
    grad_branch = jax.vjp(gelu_tanh, branch)[1](grad_mixed * states)[0].astype(BF16)
    grad_branch_proj = unswap_columns(sum_rows(normed, grad_branch, branch_proj.shape[0]))
    grad_states = grad_mixed * gate_values
    next_decays = jnp.concatenate([decays[1:], jnp.ones_like(decays[:1])], axis=0)
    back_cum, back_local = scan(next_decays, grad_states, True)
    incoming = jnp.zeros_like(back_local[0])
    for _ in range(x_count - 1):
        incoming = shifted(decays[0] * (back_cum[0] * incoming + back_local[0]), "x", -1)
    carried = back_local + back_cum * incoming
    previous = jnp.concatenate([state_in[None], states[:-1]], axis=0)
    drive_grad = carried * conv_value
    grad_log = carried * previous * decays - drive_grad * inlets * decays * decays / scaling
    grad_recur_pre = grad_log * (-8.0 * channel_rate) * recurrence * (1.0 - recurrence)
    grad_inlet_pre = drive_grad * scaling * inlets * (1.0 - inlets)
    grad_param = jnp.sum(grad_log * (-8.0 * recurrence), axis=0) * jax.nn.sigmoid(param_wide)
    rounded_recur = grad_recur_pre.astype(BF16)
    rounded_inlet = grad_inlet_pre.astype(BF16)
    grad_gates_here = jnp.concatenate(
        [head_outer(conv_low, rounded_recur), head_outer(conv_low, rounded_inlet)], axis=1
    )
    grad_gates = sum_half(
        lambda place: lax.dynamic_slice_in_dim(grad_gates_here, place * per_x, per_x, 0), channels
    )
    grad_conv = (
        carried * scaling * inlets
        + head_product_back(rounded_recur, recur_full)
        + head_product_back(rounded_inlet, inlet_full)
    )
    ahead = shifted(grad_conv[:3], "x", -1)
    extended_back = jnp.concatenate([grad_conv, ahead], axis=0)
    grad_inner = kernel_wide[0] * extended_back[0:rows]
    for offset in range(1, 4):
        grad_inner = grad_inner + kernel_wide[offset] * extended_back[offset : offset + rows]
    grad_inner = grad_inner.astype(BF16)
    grad_input_proj = unswap_columns(sum_rows(normed, grad_inner, input_proj.shape[0]))
    grad_kernel = jnp.stack(
        [
            jnp.sum(grad_conv * extended_wide[3 - offset : 3 - offset + rows], axis=0)
            for offset in range(4)
        ],
        axis=0,
    )
    grad_normed = mixer_order_back(
        pair_sum(dot_t(grad_inner, input_full) + dot_t(grad_branch, branch_full))
    )
    grad_token_norm, grad_gain_mixer = norm_backward(grad_normed, scaled_one, factor_one, gain_one)
    grad_tokens = (grad_middle + grad_token_norm)[None]

    channel_sums = jnp.concatenate(
        [
            grad_kernel,
            jnp.stack(
                [
                    jnp.sum(grad_conv, axis=0),
                    jnp.sum(grad_recur_pre, axis=0),
                    jnp.sum(grad_inlet_pre, axis=0),
                    grad_param,
                ]
            ),
        ],
        axis=0,
    )
    channel_sums = channel_sums.reshape(8, half, channels).transpose(1, 0, 2)
    everyones = lax.dynamic_update_slice_in_dim(
        jnp.zeros((2 * half, 8, channels), F32), channel_sums, core * half, 0
    ).reshape(2 * half, 8 * channels)
    gain_sums = jnp.stack([grad_gain_mixer, grad_gain_feed]).reshape(2, 2 * half, gain_width)
    everyones = jnp.concatenate(
        [everyones, gain_sums.transpose(1, 0, 2).reshape(2 * half, 2 * gain_width)], axis=1
    )
    sums = jnp.sum(lax.all_to_all(everyones, EVERY, 0, 0), axis=0)
    by_channel = sums[: 8 * channels].reshape(8, channels)
    by_gain = sums[8 * channels :].reshape(2, gain_width)
    return (
        output,
        grad_tokens,
        grad_input_proj,
        grad_branch_proj,
        grad_output,
        grad_gates[:, :HB],
        grad_gates[:, HB:],
        by_channel[:4],
        by_channel[4],
        by_channel[5],
        by_channel[6],
        by_channel[7],
        by_gain[0],
        by_gain[1],
        feed_grad_gate,
        feed_grad_up,
        feed_grad_down,
    )


def solution(mesh):
    seq, batch = mesh.shape["seq"], mesh.shape["batch"]
    fine = Mesh(mesh.devices.reshape(seq // 2, 2, batch // 4, 2, 2), EVERY)
    sequences, places = ("zh", "zl", "y"), ("x", "core")
    rows = P(sequences, places, None)
    spread_rows, spread_columns, spread_all = P(EVERY, None), P(None, EVERY), P(EVERY)
    feed = P(sequences, places)
    feed_back = P(places, sequences)
    in_specs = (
        (rows, P(sequences), rows)
        + (spread_rows,) * 5
        + (spread_columns,)
        + (spread_all,) * 6
        + (feed, feed, feed_back)
    )
    out_specs = (
        (rows, rows)
        + (spread_rows,) * 5
        + (spread_columns,)
        + (spread_all,) * 6
        + (feed, feed, feed_back)
    )
    return jax.shard_map(
        on_device, mesh=fine, in_specs=in_specs, out_specs=out_specs, check_vma=False
    )
```
